512 devices in a mesh: section: 32 (over x, y), patch: 16 (over z, core).
Axes of the slice: x: 4, y: 8, z: 8, core: 2. Of those that a mesh axis runs over, the one named last changes fastest.
Arguments:
- previous: bfloat16 [32, 256, 2048], P('section', 'patch'), may hold values from -6 to 6
- stale_keys: bfloat16 [32, 2, 256, 2048], P('section'), may hold values from -12 to 12
- stale_values: bfloat16 [32, 2, 256, 2048], P('section'), may hold values from -6 to 6
- modulation: float32 [32, 2, 3, 2048], P('section'), may hold values from -4 to 4
- q_gain: float32 [32, 2, 128], P('section'), as said below
- k_gain: float32 [32, 2, 128], P('section'), as said below
- blocks: int32 [32], P('section'), may hold values from 1 to 2, as said below
- refresh: int32 [32, 16], P('section'), may hold values from 0 to 1, as said below
Outputs:
- mixed: float32 [32, 256, 2048], P('section', 'patch')
The draws below stay inside these ranges and needn't reach their ends.
Inputs may be any that keep to these rules, and one draw needn't show every extreme that they name: Every section runs 1 to 2 blocks and some section runs 2. `refresh`: in every section exactly 4 patches have 1, the others 0. `q_gain`: real gains. `k_gain`: real gains.
All inputs are finite; a program needn't handle non-finite values.
Results may differ from the reference program's by a relative error of at most 0.008.
The reference program's roundings to bfloat16 on the way (of `weights`) count: a program that leaves them out, or rounds other values in their place, can miss the bound.
Values may be sent and summed in bfloat16 or wider, within the bound.
A program may use at most 64 MiB of HBM per device.

```python
import math
import jax
import jax.numpy as jnp
from jax import lax

HEAD = 128
HEADS = 16
D = 2048
MAXB = 2
TOK_DEV = 16
SECTIONS = 32
PATCHES = 16
TOKENS = 256
REFRESHED = 4


def draw_q_gain(key, part):
    key = jax.random.fold_in(key, 3)
    return 2.0 * jax.random.normal(key, (SECTIONS, MAXB, HEAD), jnp.float32)


def draw_k_gain(key, part):
    key = jax.random.fold_in(key, 4)
    return 2.0 * jax.random.normal(key, (SECTIONS, MAXB, HEAD), jnp.float32)


def draw_blocks(key, part):
    key = jax.random.fold_in(key, 1)
    counts = jax.random.randint(key, (SECTIONS,), 1, MAXB + 1)
    chosen = jax.random.randint(jax.random.fold_in(key, 2), (), 0, SECTIONS)
    return counts.at[chosen].set(MAXB).astype(jnp.int32)


def draw_refresh(key, part):
    key = jax.random.fold_in(key, 2)
    row_keys = jax.random.split(key, SECTIONS)
    orders = jax.vmap(lambda row_key: jax.random.permutation(row_key, PATCHES))(row_keys)
    return (orders < REFRESHED).astype(jnp.int32)


def block_levels(own_key, dims, pieces, least, largest):
    def one(dim, blocks):
        draws = jax.random.uniform(jax.random.fold_in(jax.random.fold_in(own_key, 6), dim), (blocks,), jnp.float32, least / len(pieces), largest / len(pieces))
        return jnp.repeat(jnp.exp(draws), dims[dim] // blocks).reshape((-1,) + (1,) * (len(dims) - dim - 1))

    loudness = one(*pieces[0])
    for cut in pieces[1:]:
        loudness = loudness * one(*cut)
    return loudness


def normal_values(key, dims, deviation, most, pieces=(), dtype=jnp.bfloat16):
    array = jax.random.normal(key, dims, jnp.float32) * deviation
    if len(pieces) > 0:
        array = block_levels(key, dims, pieces, -0.22, 0.18) * array
    return jnp.clip(array, min=-most, max=most).astype(dtype)


def setup_inputs(seed: int = 0) -> dict:
    arg_keys = jax.random.split(jax.random.key(seed), 9)
    return {
        "previous": normal_values(arg_keys[0], (SECTIONS, TOKENS, D), 1.0, 6.0, ((0, 32), (1, 16))),
        "stale_keys": normal_values(arg_keys[1], (SECTIONS, MAXB, TOKENS, D), 2.0, 12.0, ((0, 32),)),
        "stale_values": normal_values(arg_keys[2], (SECTIONS, MAXB, TOKENS, D), 1.0, 6.0, ((0, 32),)),
        "modulation": normal_values(arg_keys[3], (SECTIONS, MAXB, 3, D), 0.7, 4.0, ((0, 32),), jnp.float32),
        "q_gain": draw_q_gain(jax.random.fold_in(arg_keys[8], 71), 0),
        "k_gain": draw_k_gain(jax.random.fold_in(arg_keys[8], 71), 0),
        "blocks": draw_blocks(jax.random.fold_in(arg_keys[8], 71), 0),
        "refresh": draw_refresh(jax.random.fold_in(arg_keys[8], 71), 0),
    }


epsilon = 1e-06

def rms_scale(values_in):
    return values_in * lax.rsqrt(lax.optimization_barrier(jnp.mean(values_in * values_in, axis=-1, keepdims=True)) + epsilon)

def section_pass(inputs):
    state_in, stale_k, stale_v, modulate, q_scale, k_scale, block_count, flags = inputs
    state = state_in.astype(jnp.float32)
    fresh_rows = jnp.repeat(flags, TOK_DEV) > 0
    for number in range(MAXB):
        current = state
        modded = rms_scale(current) * (1.0 + modulate[number, 1]) + modulate[number, 0]
        normed = rms_scale(modded.reshape(TOKENS, HEADS, HEAD))
        query = (normed * q_scale[number] * (1.0 / math.sqrt(HEAD))).astype(jnp.bfloat16)
        fresh_k = (normed * k_scale[number]).astype(jnp.bfloat16).reshape(TOKENS, D)
        fresh_v = modded.astype(jnp.bfloat16)
        all_keys = jnp.where(fresh_rows[:, None], fresh_k, stale_k[number]).reshape(TOKENS, HEADS, HEAD)
        all_values = jnp.where(fresh_rows[:, None], fresh_v, stale_v[number]).reshape(TOKENS, HEADS, HEAD)
        scores = jnp.einsum('qhd,khd->hqk', query.astype(jnp.float32), all_keys.astype(jnp.float32))
        raised = jnp.exp(scores - lax.optimization_barrier(jnp.max(scores, axis=-1, keepdims=True)))
        weights = (raised / lax.optimization_barrier(jnp.sum(raised, axis=-1, keepdims=True))).astype(jnp.bfloat16)
        attended = jnp.einsum('hqk,khd->qhd', weights.astype(jnp.float32), all_values.astype(jnp.float32))
        attended = attended.reshape(TOKENS, D)
        updated = current + modulate[number, 2] * attended
        state = jnp.where(number < block_count, updated, state)
    return state

def reference(previous, stale_keys, stale_values, modulation, q_gain, k_gain, blocks, refresh):
    incoming = jnp.roll(previous, 1, axis=0)
    return lax.map(section_pass, (incoming, stale_keys, stale_values, modulation, q_gain, k_gain, blocks, refresh))
```

```python
import functools
import math

import jax
import jax.numpy as jnp
from jax import lax
from jax.experimental import pallas as pl
from jax.experimental.pallas import tpu as pltpu
from jax.sharding import PartitionSpec as P

epsilon = 1e-06
VMEM_BYTES = 60 * 2**20
MESH = pl.DeviceIdType.MESH


def spread_order(count):
    chips = count // 2
    order = []
    for distance in range(chips // 2, 0, -1):
        order.append(distance)
        if chips - distance != distance:
            order.append(chips - distance)
    order.append(0)
    return [(2 * step, flip) for step in order for flip in (0, 1)]


def kernel(
    sections, patches, previous, stale_k, stale_v, modulation, q_gain, k_gain, blocks, refresh, out,
    own_rows, own_inv, state_in, inv_in, cache_k, cache_v, mod, qg, kg, flags, count,
    own_sums, sums_in, result, load_sem, send_sem, recv_sem,
):
    section = lax.axis_index("section")
    patch = lax.axis_index("patch")
    after = lax.rem(section + 1, sections)
    before = lax.rem(section + sections - 1, sections)
    tok_rows, width = own_rows.shape
    tokens, head = state_in.shape
    column = pl.ds(pl.multiple_of(patch * head, head), head)
    rows_here = pl.ds(pl.multiple_of(patch * tok_rows, tok_rows), tok_rows)

    partners = []
    for step, flip in spread_order(patches):
        chip = lax.rem(patch // 2 * 2 + step, patches)
        core = lax.rem(patch + flip, 2)
        partners.append(chip + core)

    barrier = pltpu.get_barrier_semaphore()
    for partner in partners:
        pl.semaphore_signal(
            barrier, inc=1, device_id={"section": before, "patch": partner}, device_id_type=MESH
        )

    loads = [
        pltpu.make_async_copy(previous.at[0], own_rows, load_sem.at[0]),
        pltpu.make_async_copy(stale_k.at[0, :, :, column], cache_k, load_sem.at[1]),
        pltpu.make_async_copy(stale_v.at[0, :, :, column], cache_v, load_sem.at[2]),
        pltpu.make_async_copy(modulation.at[0, :, :, column], mod, load_sem.at[3]),
        pltpu.make_async_copy(q_gain.at[0], qg, load_sem.at[4]),
        pltpu.make_async_copy(k_gain.at[0], kg, load_sem.at[5]),
        pltpu.make_async_copy(refresh, flags, load_sem.at[7]),
        pltpu.make_async_copy(blocks, count, load_sem.at[8]),
    ]
    for load in loads:
        load.start()

    lane = lax.broadcasted_iota(jnp.int32, (tok_rows, head), 1)
    row = lax.broadcasted_iota(jnp.int32, (tok_rows, head), 0)
    loads[0].wait()
    rows = own_rows[...].astype(jnp.float32)
    inverse = lax.rsqrt(jnp.mean(rows * rows, axis=-1, keepdims=True) + epsilon)
    own_inv[...] = jnp.sum(jnp.where(lane == row, inverse, 0.0), axis=0, keepdims=True)

    pl.semaphore_wait(barrier, patches)

    sends = []
    for partner in partners:
        target = {"section": after, "patch": partner}
        sends.append(pltpu.make_async_remote_copy(
            src_ref=own_inv, dst_ref=inv_in.at[patch], send_sem=send_sem.at[0], recv_sem=recv_sem.at[0],
            device_id=target, device_id_type=MESH,
        ))
        sends.append(pltpu.make_async_remote_copy(
            src_ref=own_rows.at[:, pl.ds(pl.multiple_of(partner * head, head), head)],
            dst_ref=state_in.at[rows_here, :], send_sem=send_sem.at[1], recv_sem=recv_sem.at[1],
            device_id=target, device_id_type=MESH,
        ))
    for send in sends:
        send.start()

    for load in loads[1:]:
        load.wait()
    flag_lane = lax.broadcasted_iota(jnp.int32, (tokens, patches), 1)
    flag_row = lax.broadcasted_iota(jnp.int32, (tokens, patches), 0)
    fresh = jnp.sum(
        jnp.where(flag_lane == flag_row // tok_rows, flags[...].astype(jnp.float32), 0.0), axis=-1, keepdims=True
    ) > 0.5

    def block(state, inverse, number):
        modded = state * inverse * (1.0 + mod[1, number:number + 1]) + mod[0, number:number + 1]
        normed = modded * lax.rsqrt(jnp.mean(modded * modded, axis=-1, keepdims=True) + epsilon)
        query = (normed * qg[number:number + 1] * (1.0 / math.sqrt(head))).astype(jnp.bfloat16)
        fresh_k = normed * kg[number:number + 1]
        all_keys = jnp.where(fresh, fresh_k, cache_k[number].astype(jnp.float32)).astype(jnp.bfloat16)
        all_values = jnp.where(fresh, modded, cache_v[number].astype(jnp.float32)).astype(jnp.bfloat16)
        scores = lax.dot_general(
            query, all_keys, (((1,), (1,)), ((), ())), preferred_element_type=jnp.float32
        )
        raised = jnp.exp(scores - jnp.max(scores, axis=-1, keepdims=True))
        weights = (raised / jnp.sum(raised, axis=-1, keepdims=True)).astype(jnp.bfloat16)
        attended = jnp.dot(weights, all_values, preferred_element_type=jnp.float32)
        updated = state + mod[2, number:number + 1] * attended
        return jnp.where(count[...] > number, updated, state)

    pltpu.make_async_copy(inv_in, inv_in, recv_sem.at[0]).wait()
    pltpu.make_async_copy(state_in, state_in, recv_sem.at[1]).wait()
    state = state_in[...].astype(jnp.float32)
    spread = jnp.broadcast_to(inv_in[...], (patches, tok_rows, head))
    inverse = jnp.sum(jnp.where((lane == row)[None], spread, 0.0), axis=-1, keepdims=True).reshape(tokens, 1)
    state = block(state, inverse, 0)

    halves = tokens // head
    lanes = lax.broadcasted_iota(jnp.int32, (head, head), 1)
    diagonal = (lanes == lax.broadcasted_iota(jnp.int32, (head, head), 0))[None]
    sums = jnp.sum(state * state, axis=-1, keepdims=True).reshape(halves, head, 1)
    own_sums[...] = jnp.sum(jnp.where(diagonal, sums, 0.0), axis=1)
    for partner in partners[:-2] + partners[-1:]:
        send = pltpu.make_async_remote_copy(
            src_ref=own_sums, dst_ref=sums_in.at[patch], send_sem=send_sem.at[2], recv_sem=recv_sem.at[2],
            device_id={"patch": partner}, device_id_type=MESH,
        )
        send.start()
    sums_in[patch] = own_sums[...]
    others = sums_in.at[pl.ds(0, patches - 1)]
    pltpu.make_async_copy(others, others, recv_sem.at[2]).wait()
    total = jnp.sum(sums_in[...], axis=0)
    spread = jnp.broadcast_to(total[:, None, :], (halves, head, head))
    total = jnp.sum(jnp.where(diagonal, spread, 0.0), axis=-1, keepdims=True).reshape(tokens, 1)
    inverse = lax.rsqrt(total * (1.0 / width) + epsilon)
    state = block(state, inverse, 1)

    result[...] = state.astype(result.dtype)
    for partner in partners[:-2] + partners[-1:]:
        send = pltpu.make_async_remote_copy(
            src_ref=result.at[pl.ds(pl.multiple_of(partner * tok_rows, tok_rows), tok_rows), :],
            dst_ref=out.at[:, column], send_sem=send_sem.at[3], recv_sem=recv_sem.at[3],
            device_id={"patch": partner}, device_id_type=MESH,
        )
        send.start()
    own = pltpu.make_async_copy(result.at[rows_here, :], out.at[:, column], load_sem.at[6])
    own.start()
    own.wait()
    pltpu.make_async_copy(inv_in, inv_in, send_sem.at[0]).wait()
    pltpu.make_async_copy(state_in, state_in, send_sem.at[1]).wait()
    pltpu.make_async_copy(others, others, send_sem.at[2]).wait()
    rest = result.at[pl.ds(0, tokens - tok_rows), :]
    pltpu.make_async_copy(rest, rest, send_sem.at[3]).wait()
    pltpu.make_async_copy(rest, rest, recv_sem.at[3]).wait()


def per_device(previous, stale_keys, stale_values, modulation, q_gain, k_gain, blocks, refresh):
    sections = lax.axis_size("section")
    patches = lax.axis_size("patch")
    _, tok_rows, width = previous.shape
    _, layers, tokens, _ = stale_keys.shape
    head = q_gain.shape[-1]
    anywhere = pl.BlockSpec(memory_space=pl.ANY)
    mixed = pl.pallas_call(
        functools.partial(kernel, sections, patches),
        out_shape=jax.ShapeDtypeStruct((tok_rows, width), jnp.bfloat16),
        in_specs=[anywhere] * 8,
        out_specs=pl.BlockSpec(memory_space=pltpu.VMEM),
        scratch_shapes=[
            pltpu.VMEM((tok_rows, width), jnp.bfloat16),
            pltpu.VMEM((1, head), jnp.float32),
            pltpu.VMEM((tokens, head), jnp.bfloat16),
            pltpu.VMEM((patches, 1, head), jnp.float32),
            pltpu.VMEM((layers, tokens, head), jnp.bfloat16),
            pltpu.VMEM((layers, tokens, head), jnp.bfloat16),
            pltpu.VMEM((3, layers, head), jnp.float32),
            pltpu.VMEM((layers, head), jnp.float32),
            pltpu.VMEM((layers, head), jnp.float32),
            pltpu.VMEM((1, patches), jnp.int32),
            pltpu.VMEM((1, 1), jnp.int32),
            pltpu.VMEM((tokens // head, head), jnp.float32),
            pltpu.VMEM((patches, tokens // head, head), jnp.float32),
            pltpu.VMEM((tokens, head), jnp.bfloat16),
            pltpu.SemaphoreType.DMA((9,)),
            pltpu.SemaphoreType.DMA((4,)),
            pltpu.SemaphoreType.DMA((4,)),
        ],
        compiler_params=pltpu.CompilerParams(collective_id=0, has_side_effects=True, vmem_limit_bytes=VMEM_BYTES),
    )(previous, stale_keys, stale_values, jnp.swapaxes(modulation, 1, 2), q_gain, k_gain, blocks[None], refresh)
    return mixed.astype(jnp.float32)[None]


def solution(mesh):
    placed = (
        P("section", "patch", None),
        P("section", None, None, None),
        P("section", None, None, None),
        P("section", None, None, None),
        P("section", None, None),
        P("section", None, None),
        P("section"),
        P("section", None),
    )
    return jax.shard_map(
        per_device,
        mesh=mesh,
        in_specs=placed,
        out_specs=P("section", "patch", None),
        check_vma=False,
    )
```

```python
import functools
import math

import jax
import jax.numpy as jnp
from jax import lax
from jax.experimental import pallas as pl
from jax.experimental.pallas import tpu as pltpu
from jax.sharding import PartitionSpec as P

epsilon = 1e-06
VMEM_BYTES = 48 * 2**20
MESH = pl.DeviceIdType.MESH
PIECES = 2
FIRST, WORKERS = 2, 4


def kernel(
    sections, patches, head, previous, stale_k, stale_v, modulation, q_gain, k_gain, refresh, blocks, out,
    own_rows, own_inv, state_in, inv_in, cache_k, cache_v, mod, qg, kg, flags, count,
    own_sums, sums_in, result, load_sem, send_sem, recv_sem, ready_sem,
):
    section = lax.axis_index("section")
    patch = lax.axis_index("patch")
    after = lax.rem(section + 1, sections)
    before = lax.rem(section + sections - 1, sections)
    tok_rows, width = own_rows.shape
    tokens, part = state_in.shape
    share = part // PIECES
    works = jnp.logical_and(patch >= FIRST, patch < FIRST + WORKERS)
    slot = lax.rem(patch + patches - FIRST, patches)
    mine = lax.rem(slot, WORKERS)
    column = pl.ds(pl.multiple_of(mine * part, part), part)
    rows_here = pl.ds(pl.multiple_of(patch * tok_rows, tok_rows), tok_rows)

    barrier = pltpu.get_barrier_semaphore()

    def to(where, partner):
        return {"device_id": {"section": where, "patch": partner}, "device_id_type": MESH}

    loads = [
        pltpu.make_async_copy(stale_k.at[0, :, :, column], cache_k, load_sem.at[1]),
        pltpu.make_async_copy(stale_v.at[0, :, :, column], cache_v, load_sem.at[2]),
        pltpu.make_async_copy(modulation.at[0, :, :, column], mod, load_sem.at[3]),
        pltpu.make_async_copy(q_gain.at[0], qg, load_sem.at[4]),
        pltpu.make_async_copy(k_gain.at[0], kg, load_sem.at[5]),
        pltpu.make_async_copy(refresh, flags, load_sem.at[6]),
        pltpu.make_async_copy(blocks, count, load_sem.at[7]),
    ]
    load_rows = pltpu.make_async_copy(previous.at[0], own_rows, load_sem.at[0])
    load_rows.start()

    @pl.when(works)
    def _():
        for partner in range(patches - 1, -1, -1):
            pl.semaphore_signal(barrier, inc=1, **to(before, partner))
        for partner in range(patches - 1, -1, -1):
            @pl.when(partner != patch)
            def _():
                pl.semaphore_signal(barrier, inc=1, **to(section, partner))
        for load in loads:
            load.start()

    pl.semaphore_wait(barrier, 2 * WORKERS - works.astype(jnp.int32))

    def pass_on(piece):
        for index in range(WORKERS):
            pltpu.make_async_remote_copy(
                src_ref=previous.at[0, :, pl.ds(index * part + piece * share, share)],
                dst_ref=state_in.at[rows_here, pl.ds(piece * share, share)],
                send_sem=send_sem.at[1], recv_sem=recv_sem.at[4 + piece], **to(after, FIRST + index),
            ).start()

    pass_on(0)
    load_rows.wait()
    rows = own_rows[...].astype(jnp.float32)
    lane = lax.broadcasted_iota(jnp.int32, (tok_rows, 128), 1)
    row = lax.broadcasted_iota(jnp.int32, (tok_rows, 128), 0)
    inverse = lax.rsqrt(jnp.mean(rows * rows, axis=-1, keepdims=True) + epsilon)
    own_inv[...] = jnp.sum(jnp.where(lane == row, inverse, 0.0), axis=0, keepdims=True)
    for index in range(WORKERS):
        pltpu.make_async_remote_copy(
            src_ref=own_inv, dst_ref=inv_in.at[patch],
            send_sem=send_sem.at[0], recv_sem=recv_sem.at[0], **to(after, FIRST + index),
        ).start()
    for piece in range(1, PIECES):
        pass_on(piece)

    @pl.when(jnp.logical_not(works))
    def _():
        for index in range(WORKERS):
            pl.semaphore_signal(ready_sem, inc=1, **to(section, FIRST + index))

    @pl.when(works)
    def _():
        flag_lane = lax.broadcasted_iota(jnp.int32, (tokens, patches), 1)
        flag_row = lax.broadcasted_iota(jnp.int32, (tokens, patches), 0)
        for load in loads:
            load.wait()
        fresh = jnp.sum(
            jnp.where(flag_lane == flag_row // tok_rows, flags[...].astype(jnp.float32), 0.0), axis=-1, keepdims=True
        ) > 0.5

        def prepare(h, state, inverse, number):
            here = slice(h * head, (h + 1) * head)
            modded = state * inverse * (1.0 + mod[1, number:number + 1, here]) + mod[0, number:number + 1, here]
            normed = modded * lax.rsqrt(jnp.mean(modded * modded, axis=-1, keepdims=True) + epsilon)
            query = (normed * (qg[number:number + 1] * (1.0 / math.sqrt(head)))).astype(jnp.bfloat16)
            cached_k = cache_k[number, :, here].astype(jnp.float32)
            cached_v = cache_v[number, :, here].astype(jnp.float32)
            all_keys = jnp.where(fresh, normed * kg[number:number + 1], cached_k).astype(jnp.bfloat16)
            all_values = jnp.where(fresh, modded, cached_v).astype(jnp.bfloat16)
            return query, all_keys, all_values

        def attend(h, state, number, query, all_keys, all_values):
            here = slice(h * head, (h + 1) * head)
            scores = lax.dot_general(
                query, all_keys, (((1,), (1,)), ((), ())), preferred_element_type=jnp.float32
            )
            raised = jnp.exp(scores - jnp.max(scores, axis=-1, keepdims=True))
            total = jnp.sum(raised, axis=-1, keepdims=True)
            weights = (raised * (1.0 / total)).astype(jnp.bfloat16)
            attended = jnp.dot(weights, all_values, preferred_element_type=jnp.float32)
            updated = state + mod[2, number:number + 1, here] * attended
            return jnp.where(count[...] > number, updated, state)

        pltpu.make_async_copy(inv_in, inv_in, recv_sem.at[0]).wait()
        spread = jnp.broadcast_to(inv_in[...], (patches, tok_rows, 128))
        inverse = jnp.sum(jnp.where((lane == row)[None], spread, 0.0), axis=-1, keepdims=True).reshape(tokens, 1)
        heads = part // head
        middle = []
        for piece in range(PIECES):
            arrived = state_in.at[:, pl.ds(piece * share, share)]
            pltpu.make_async_copy(arrived, arrived, recv_sem.at[4 + piece]).wait()
            for h in range(piece * heads // PIECES, (piece + 1) * heads // PIECES):
                state = state_in[:, h * head:(h + 1) * head].astype(jnp.float32)
                middle.append(attend(h, state, 0, *prepare(h, state, inverse, 0)))

        halves = tokens // 128
        lanes = lax.broadcasted_iota(jnp.int32, (128, 128), 1)
        diagonal = (lanes == lax.broadcasted_iota(jnp.int32, (128, 128), 0))[None]
        squares = functools.reduce(jnp.add, [state * state for state in middle])
        sums = jnp.sum(squares, axis=-1, keepdims=True).reshape(halves, 128, 1)
        own_sums[...] = jnp.sum(jnp.where(diagonal, sums, 0.0), axis=1)
        for step in range(1, WORKERS):
            pltpu.make_async_remote_copy(
                src_ref=own_sums, dst_ref=sums_in.at[slot], send_sem=send_sem.at[2], recv_sem=recv_sem.at[2],
                **to(section, FIRST + lax.rem(slot + step, WORKERS)),
            ).start()
        sums_in[slot] = own_sums[...]
        others = sums_in.at[pl.ds(0, WORKERS - 1)]
        pltpu.make_async_copy(others, others, recv_sem.at[2]).wait()
        total = jnp.sum(sums_in[...], axis=0)
        spread = jnp.broadcast_to(total[:, None, :], (halves, 128, 128))
        total = jnp.sum(jnp.where(diagonal, spread, 0.0), axis=-1, keepdims=True).reshape(tokens, 1)
        inverse = lax.rsqrt(total * (1.0 / width) + epsilon)

        pl.semaphore_wait(ready_sem, patches - WORKERS)

        def give(partner, first, last):
            rows_there = pl.ds(partner * tok_rows, tok_rows)
            source = result.at[rows_there, pl.ds(first * head, (last - first) * head)]
            target = out.at[:, pl.ds(pl.multiple_of(mine * part + first * head, head), (last - first) * head)]

            def send():
                pltpu.make_async_remote_copy(
                    src_ref=source, dst_ref=target, send_sem=send_sem.at[3], recv_sem=recv_sem.at[3],
                    **to(section, partner),
                ).start()

            if FIRST <= partner < FIRST + WORKERS:
                pl.when(partner != patch)(send)

                @pl.when(partner == patch)
                def _():
                    pltpu.make_async_copy(source, target, load_sem.at[8]).start()
            else:
                send()

        ready = [prepare(h, middle[h], inverse, 1) for h in range(heads)]
        for first, last in ((0, tokens // 2), (tokens // 2, tokens)):
            for h in range(heads):
                query, all_keys, all_values = ready[h]
                state = attend(h, middle[h][first:last], 1, query[first:last], all_keys, all_values)
                result[first:last, h * head:(h + 1) * head] = state.astype(result.dtype)
                if first == 0:
                    for partner in range(FIRST):
                        give(partner, h, h + 1)
            for partner in range(max(first // tok_rows, FIRST), last // tok_rows):
                give(partner, 0, heads)
        pltpu.make_async_copy(result.at[rows_here, :], out.at[:, column], load_sem.at[8]).wait()
        pltpu.make_async_copy(others, others, send_sem.at[2]).wait()
        rest = result.at[pl.ds(0, tokens - tok_rows), :]
        pltpu.make_async_copy(rest, rest, send_sem.at[3]).wait()
        arriving = out.at[:, pl.ds(0, width - part)]
        pltpu.make_async_copy(arriving, arriving, recv_sem.at[3]).wait()

    sent = inv_in.at[pl.ds(0, WORKERS)]
    pltpu.make_async_copy(sent, sent, send_sem.at[0]).wait()
    pltpu.make_async_copy(own_rows, own_rows, send_sem.at[1]).wait()

    @pl.when(jnp.logical_not(works))
    def _():
        pltpu.make_async_copy(out, out, recv_sem.at[3]).wait()


def per_device(previous, stale_keys, stale_values, modulation, q_gain, k_gain, blocks, refresh):
    sections = lax.axis_size("section")
    patches = lax.axis_size("patch")
    _, tok_rows, width = previous.shape
    _, layers, tokens, _ = stale_keys.shape
    head = q_gain.shape[-1]
    part = width // WORKERS
    anywhere = pl.BlockSpec(memory_space=pl.ANY)
    operands = (previous, stale_keys, stale_values, jnp.swapaxes(modulation, 1, 2), q_gain, k_gain, refresh)
    stay = [pltpu.with_memory_space_constraint(operand, pltpu.HBM) for operand in operands]
    mixed = pl.pallas_call(
        functools.partial(kernel, sections, patches, head),
        out_shape=pltpu.VMEM((tok_rows, width), jnp.bfloat16),
        in_specs=[anywhere] * 8,
        out_specs=pl.BlockSpec(memory_space=pltpu.VMEM),
        scratch_shapes=[
            pltpu.VMEM((tok_rows, width), jnp.bfloat16),
            pltpu.VMEM((1, 128), jnp.float32),
            pltpu.VMEM((tokens, part), jnp.bfloat16),
            pltpu.VMEM((patches, 1, 128), jnp.float32),
            pltpu.VMEM((layers, tokens, part), jnp.bfloat16),
            pltpu.VMEM((layers, tokens, part), jnp.bfloat16),
            pltpu.VMEM((3, layers, part), jnp.float32),
            pltpu.VMEM((layers, head), jnp.float32),
            pltpu.VMEM((layers, head), jnp.float32),
            pltpu.VMEM((1, patches), jnp.int32),
            pltpu.VMEM((1, 1), jnp.int32),
            pltpu.VMEM((tokens // 128, 128), jnp.float32),
            pltpu.VMEM((WORKERS, tokens // 128, 128), jnp.float32),
            pltpu.VMEM((tokens, part), jnp.bfloat16),
            pltpu.SemaphoreType.DMA((9,)),
            pltpu.SemaphoreType.DMA((4,)),
            pltpu.SemaphoreType.DMA((4 + PIECES,)),
            pltpu.SemaphoreType.REGULAR,
        ],
        compiler_params=pltpu.CompilerParams(
            collective_id=0, has_side_effects=True, vmem_limit_bytes=VMEM_BYTES
        ),
    )(*stay, blocks[None])
    return mixed.astype(jnp.float32)[None]


def solution(mesh):
    placed = (
        P("section", "patch", None),
        P("section", None, None, None),
        P("section", None, None, None),
        P("section", None, None, None),
        P("section", None, None),
        P("section", None, None),
        P("section"),
        P("section", None),
    )
    return jax.shard_map(
        per_device,
        mesh=mesh,
        in_specs=placed,
        out_specs=P("section", "patch", None),
        check_vma=False,
    )
```

```python
import functools
import math

import jax
import jax.numpy as jnp
from jax import lax
from jax.experimental import pallas as pl
from jax.experimental.pallas import tpu as pltpu
from jax.sharding import PartitionSpec as P

epsilon = 1e-06
VMEM_BYTES = 48 * 2**20
MESH = pl.DeviceIdType.MESH
PIECES = 2
STEPS = ((0, 256, (1, 3, 2, 0, 4, 5, 6, 7, 14, 15, 8, 9, 12, 13, 10, 11)),)
FIRST, WORKERS = 2, 4


def kernel(
    sections, patches, head, previous, stale_k, stale_v, modulation, q_gain, k_gain, refresh, blocks, out,
    own_rows, own_inv, state_in, inv_in, cache_k, cache_v, mod, qg, kg, flags, count,
    own_sums, sums_in, result, load_sem, send_sem, recv_sem, ready_sem,
):
    section = lax.axis_index("section")
    patch = lax.axis_index("patch")
    after = lax.rem(section + 1, sections)
    before = lax.rem(section + sections - 1, sections)
    tok_rows, width = own_rows.shape
    tokens, part = state_in.shape
    share = part // PIECES
    works = jnp.logical_and(patch >= FIRST, patch < FIRST + WORKERS)
    slot = lax.rem(patch + patches - FIRST, patches)
    mine = lax.rem(slot, WORKERS)
    column = pl.ds(pl.multiple_of(mine * part, part), part)
    rows_here = pl.ds(pl.multiple_of(patch * tok_rows, tok_rows), tok_rows)

    barrier = pltpu.get_barrier_semaphore()

    def to(where, partner):
        return {"device_id": {"section": where, "patch": partner}, "device_id_type": MESH}

    loads = [
        pltpu.make_async_copy(stale_k.at[0, :, :, column], cache_k, load_sem.at[1]),
        pltpu.make_async_copy(stale_v.at[0, :, :, column], cache_v, load_sem.at[2]),
        pltpu.make_async_copy(modulation.at[0, :, :, column], mod, load_sem.at[3]),
        pltpu.make_async_copy(q_gain.at[0], qg, load_sem.at[4]),
        pltpu.make_async_copy(k_gain.at[0], kg, load_sem.at[5]),
        pltpu.make_async_copy(refresh, flags, load_sem.at[6]),
        pltpu.make_async_copy(blocks, count, load_sem.at[7]),
    ]
    load_rows = pltpu.make_async_copy(previous.at[0], own_rows, load_sem.at[0])

    @pl.when(works)
    def _():
        for partner in range(patches - 1, -1, -1):
            pl.semaphore_signal(barrier, inc=1, **to(before, partner))
        for partner in range(patches - 1, -1, -1):
            @pl.when(partner != patch)
            def _():
                pl.semaphore_signal(barrier, inc=1, **to(section, partner))
        for load in loads:
            load.start()

    pl.semaphore_wait(barrier, 2 * WORKERS - works.astype(jnp.int32))

    def pass_on(piece):
        for index in range(WORKERS):
            pltpu.make_async_remote_copy(
                src_ref=previous.at[0, :, pl.ds(index * part + piece * share, share)],
                dst_ref=state_in.at[rows_here, pl.ds(piece * share, share)],
                send_sem=send_sem.at[1], recv_sem=recv_sem.at[4 + piece], **to(after, FIRST + index),
            ).start()

    pass_on(0)
    load_rows.start()
    load_rows.wait()
    rows = own_rows[...].astype(jnp.float32)
    lane = lax.broadcasted_iota(jnp.int32, (tok_rows, 128), 1)
    row = lax.broadcasted_iota(jnp.int32, (tok_rows, 128), 0)
    inverse = lax.rsqrt(jnp.mean(rows * rows, axis=-1, keepdims=True) + epsilon)
    own_inv[...] = jnp.sum(jnp.where(lane == row, inverse, 0.0), axis=0, keepdims=True)
    for index in range(WORKERS):
        pltpu.make_async_remote_copy(
            src_ref=own_inv, dst_ref=inv_in.at[patch],
            send_sem=send_sem.at[0], recv_sem=recv_sem.at[0], **to(after, FIRST + index),
        ).start()
    for piece in range(1, PIECES):
        pass_on(piece)

    @pl.when(jnp.logical_not(works))
    def _():
        for index in range(WORKERS):
            pl.semaphore_signal(ready_sem, inc=1, **to(section, FIRST + index))

    @pl.when(works)
    def _():
        flag_lane = lax.broadcasted_iota(jnp.int32, (tokens, patches), 1)
        flag_row = lax.broadcasted_iota(jnp.int32, (tokens, patches), 0)
        for load in loads:
            load.wait()
        fresh = jnp.sum(
            jnp.where(flag_lane == flag_row // tok_rows, flags[...].astype(jnp.float32), 0.0), axis=-1, keepdims=True
        ) > 0.5

        def prepare(numbers, states, inverse, number):
            modded = []
            for h, state in zip(numbers, states):
                here = slice(h * head, (h + 1) * head)
                modded.append(state * inverse * (1.0 + mod[1, number:number + 1, here]) + mod[0, number:number + 1, here])
            squared = [jnp.mean(rows * rows, axis=-1, keepdims=True) for rows in modded]
            ready = []
            for h, rows, square in zip(numbers, modded, squared):
                here = slice(h * head, (h + 1) * head)
                normed = rows * lax.rsqrt(square + epsilon)
                query = (normed * (qg[number:number + 1] * (1.0 / math.sqrt(head)))).astype(jnp.bfloat16)
                cached_k = cache_k[number, :, here].astype(jnp.float32)
                cached_v = cache_v[number, :, here].astype(jnp.float32)
                all_keys = jnp.where(fresh, normed * kg[number:number + 1], cached_k).astype(jnp.bfloat16)
                all_values = jnp.where(fresh, rows, cached_v).astype(jnp.bfloat16)
                ready.append((query, all_keys, all_values))
            return ready

        def attend(numbers, states, number, ready, first, last):
            scores = [
                lax.dot_general(
                    query[first:last], all_keys, (((1,), (1,)), ((), ())), preferred_element_type=jnp.float32
                )
                for query, all_keys, _ in ready
            ]
            largest = [jnp.max(score, axis=-1, keepdims=True) for score in scores]
            raised = [jnp.exp(score - most) for score, most in zip(scores, largest)]
            scale = [1.0 / jnp.sum(terms, axis=-1, keepdims=True) for terms in raised]
            weights = [(terms * one).astype(jnp.bfloat16) for terms, one in zip(raised, scale)]
            attended = [
                jnp.dot(weight, all_values, preferred_element_type=jnp.float32)
                for weight, (_, _, all_values) in zip(weights, ready)
            ]
            runs = count[...] > number
            updated = []
            for h, state, change in zip(numbers, states, attended):
                rows = state[first:last]
                moved = rows + mod[2, number:number + 1, h * head:(h + 1) * head] * change
                updated.append(jnp.where(runs, moved, rows))
            return updated

        pltpu.make_async_copy(inv_in, inv_in, recv_sem.at[0]).wait()
        spread = jnp.broadcast_to(inv_in[...], (patches, tok_rows, 128))
        inverse = jnp.sum(jnp.where((lane == row)[None], spread, 0.0), axis=-1, keepdims=True).reshape(tokens, 1)
        heads = part // head
        middle = []
        for piece in range(PIECES):
            arrived = state_in.at[:, pl.ds(piece * share, share)]
            pltpu.make_async_copy(arrived, arrived, recv_sem.at[4 + piece]).wait()
            numbers = range(piece * heads // PIECES, (piece + 1) * heads // PIECES)
            states = [state_in[:, h * head:(h + 1) * head].astype(jnp.float32) for h in numbers]
            middle += attend(numbers, states, 0, prepare(numbers, states, inverse, 0), 0, tokens)

        halves = tokens // 128
        lanes = lax.broadcasted_iota(jnp.int32, (128, 128), 1)
        diagonal = (lanes == lax.broadcasted_iota(jnp.int32, (128, 128), 0))[None]
        squares = functools.reduce(jnp.add, [state * state for state in middle])
        sums = jnp.sum(squares, axis=-1, keepdims=True).reshape(halves, 128, 1)
        own_sums[...] = jnp.sum(jnp.where(diagonal, sums, 0.0), axis=1)
        for step in range(1, WORKERS):
            pltpu.make_async_remote_copy(
                src_ref=own_sums, dst_ref=sums_in.at[slot], send_sem=send_sem.at[2], recv_sem=recv_sem.at[2],
                **to(section, FIRST + lax.rem(slot + step, WORKERS)),
            ).start()
        sums_in[slot] = own_sums[...]
        others = sums_in.at[pl.ds(0, WORKERS - 1)]
        pltpu.make_async_copy(others, others, recv_sem.at[2]).wait()
        total = lax.rsqrt(jnp.sum(sums_in[...], axis=0) * (1.0 / width) + epsilon)
        spread = jnp.broadcast_to(total[:, None, :], (halves, 128, 128))
        inverse = jnp.sum(jnp.where(diagonal, spread, 0.0), axis=-1, keepdims=True).reshape(tokens, 1)

        pl.semaphore_wait(ready_sem, patches - WORKERS)

        def give(partner, first, last):
            rows_there = pl.ds(partner * tok_rows, tok_rows)
            source = result.at[rows_there, pl.ds(first * head, (last - first) * head)]
            target = out.at[:, pl.ds(pl.multiple_of(mine * part + first * head, head), (last - first) * head)]

            def send():
                pltpu.make_async_remote_copy(
                    src_ref=source, dst_ref=target, send_sem=send_sem.at[3], recv_sem=recv_sem.at[3],
                    **to(section, partner),
                ).start()

            if FIRST <= partner < FIRST + WORKERS:
                pl.when(partner != patch)(send)

                @pl.when(partner == patch)
                def _():
                    pltpu.make_async_copy(source, target, load_sem.at[8]).start()
            else:
                send()

        numbers = range(heads)
        ready = prepare(numbers, middle, inverse, 1)
        for first, last, order in STEPS:
            for h, state in zip(numbers, attend(numbers, middle, 1, ready, first, last)):
                result[first:last, h * head:(h + 1) * head] = state.astype(result.dtype)
            for partner in order:
                give(partner, 0, heads)
        pltpu.make_async_copy(result.at[rows_here, :], out.at[:, column], load_sem.at[8]).wait()
        pltpu.make_async_copy(others, others, send_sem.at[2]).wait()
        rest = result.at[pl.ds(0, tokens - tok_rows), :]
        pltpu.make_async_copy(rest, rest, send_sem.at[3]).wait()
        arriving = out.at[:, pl.ds(0, width - part)]
        pltpu.make_async_copy(arriving, arriving, recv_sem.at[3]).wait()

    sent = inv_in.at[pl.ds(0, WORKERS)]
    pltpu.make_async_copy(sent, sent, send_sem.at[0]).wait()
    pltpu.make_async_copy(own_rows, own_rows, send_sem.at[1]).wait()

    @pl.when(jnp.logical_not(works))
    def _():
        pltpu.make_async_copy(out, out, recv_sem.at[3]).wait()


def per_device(previous, stale_keys, stale_values, modulation, q_gain, k_gain, blocks, refresh):
    sections = lax.axis_size("section")
    patches = lax.axis_size("patch")
    _, tok_rows, width = previous.shape
    _, layers, tokens, _ = stale_keys.shape
    head = q_gain.shape[-1]
    part = width // WORKERS
    anywhere = pl.BlockSpec(memory_space=pl.ANY)
    operands = (previous, stale_keys, stale_values, jnp.swapaxes(modulation, 1, 2), q_gain, k_gain, refresh)
    stay = [pltpu.with_memory_space_constraint(operand, pltpu.HBM) for operand in operands]
    mixed = pl.pallas_call(
        functools.partial(kernel, sections, patches, head),
        out_shape=pltpu.VMEM((tok_rows, width), jnp.bfloat16),
        in_specs=[anywhere] * 8,
        out_specs=pl.BlockSpec(memory_space=pltpu.VMEM),
        scratch_shapes=[
            pltpu.VMEM((tok_rows, width), jnp.bfloat16),
            pltpu.VMEM((1, 128), jnp.float32),
            pltpu.VMEM((tokens, part), jnp.bfloat16),
            pltpu.VMEM((patches, 1, 128), jnp.float32),
            pltpu.VMEM((layers, tokens, part), jnp.bfloat16),
            pltpu.VMEM((layers, tokens, part), jnp.bfloat16),
            pltpu.VMEM((3, layers, part), jnp.float32),
            pltpu.VMEM((layers, head), jnp.float32),
            pltpu.VMEM((layers, head), jnp.float32),
            pltpu.VMEM((1, patches), jnp.int32),
            pltpu.VMEM((1, 1), jnp.int32),
            pltpu.VMEM((tokens // 128, 128), jnp.float32),
            pltpu.VMEM((WORKERS, tokens // 128, 128), jnp.float32),
            pltpu.VMEM((tokens, part), jnp.bfloat16),
            pltpu.SemaphoreType.DMA((9,)),
            pltpu.SemaphoreType.DMA((4,)),
            pltpu.SemaphoreType.DMA((4 + PIECES,)),
            pltpu.SemaphoreType.REGULAR,
        ],
        compiler_params=pltpu.CompilerParams(
            collective_id=0, has_side_effects=True, vmem_limit_bytes=VMEM_BYTES
        ),
    )(*stay, blocks[None])
    return mixed.astype(jnp.float32)[None]


def solution(mesh):
    placed = (
        P("section", "patch", None),
        P("section", None, None, None),
        P("section", None, None, None),
        P("section", None, None, None),
        P("section", None, None),
        P("section", None, None),
        P("section"),
        P("section", None),
    )
    return jax.shard_map(
        per_device,
        mesh=mesh,
        in_specs=placed,
        out_specs=P("section", "patch", None),
        check_vma=False,
    )
```

```python
import functools
import math

import jax
import jax.numpy as jnp
from jax import lax
from jax.experimental import pallas as pl
from jax.experimental.pallas import tpu as pltpu
from jax.sharding import PartitionSpec as P

epsilon = 1e-06
VMEM_BYTES = 48 * 2**20
MESH = pl.DeviceIdType.MESH
PIECES = 2
STEPS = ((0, 256, (1, 3, 2, 0, 4, 5, 6, 7, 14, 15, 8, 9, 12, 13, 10, 11)),)
FIRST, WORKERS = 2, 4


def kernel(
    sections, patches, head, previous, stale_k, stale_v, modulation, q_gain, k_gain, refresh, blocks, out,
    own_rows, own_inv, state_in, inv_in, cache_k, cache_v, mod, qg, kg, flags, count,
    own_sums, sums_in, result, load_sem, send_sem, recv_sem, ready_sem,
):
    section = lax.axis_index("section")
    patch = lax.axis_index("patch")
    after = lax.rem(section + 1, sections)
    before = lax.rem(section + sections - 1, sections)
    tok_rows, width = own_rows.shape
    tokens, part = state_in.shape
    share = part // PIECES
    works = jnp.logical_and(patch >= FIRST, patch < FIRST + WORKERS)
    slot = lax.rem(patch + patches - FIRST, patches)
    mine = lax.rem(slot, WORKERS)
    column = pl.ds(pl.multiple_of(mine * part, part), part)
    rows_here = pl.ds(pl.multiple_of(patch * tok_rows, tok_rows), tok_rows)

    barrier = pltpu.get_barrier_semaphore()

    def to(where, partner):
        return {"device_id": {"section": where, "patch": partner}, "device_id_type": MESH}

    loads = [
        pltpu.make_async_copy(stale_k.at[0, :, :, column], cache_k, load_sem.at[1]),
        pltpu.make_async_copy(stale_v.at[0, :, :, column], cache_v, load_sem.at[2]),
        pltpu.make_async_copy(modulation.at[0, :, :, column], mod, load_sem.at[3]),
        pltpu.make_async_copy(q_gain.at[0], qg, load_sem.at[4]),
        pltpu.make_async_copy(k_gain.at[0], kg, load_sem.at[5]),
        pltpu.make_async_copy(refresh, flags, load_sem.at[6]),
        pltpu.make_async_copy(blocks, count, load_sem.at[7]),
    ]
    load_rows = pltpu.make_async_copy(previous.at[0], own_rows, load_sem.at[0])

    @pl.when(works)
    def _():
        for partner in range(patches - 1, -1, -1):
            pl.semaphore_signal(barrier, inc=1, **to(before, partner))
        for partner in range(patches - 1, -1, -1):
            @pl.when(partner != patch)
            def _():
                pl.semaphore_signal(barrier, inc=1, **to(section, partner))
        for load in loads:
            load.start()

    pl.semaphore_wait(barrier, 2 * WORKERS - works.astype(jnp.int32))

    order = range(WORKERS - 1, -1, -1)

    def pass_on(piece):
        for index in order:
            begin = pl.multiple_of(index * part + piece * share, share)
            pltpu.make_async_remote_copy(
                src_ref=previous.at[0, :, pl.ds(begin, share)],
                dst_ref=state_in.at[rows_here, pl.ds(piece * share, share)],
                send_sem=send_sem.at[1], recv_sem=recv_sem.at[4 + piece], **to(after, FIRST + index),
            ).start()

    pass_on(0)
    load_rows.start()
    load_rows.wait()
    rows = own_rows[...].astype(jnp.float32)
    lane = lax.broadcasted_iota(jnp.int32, (tok_rows, 128), 1)
    row = lax.broadcasted_iota(jnp.int32, (tok_rows, 128), 0)
    inverse = lax.rsqrt(jnp.mean(rows * rows, axis=-1, keepdims=True) + epsilon)
    own_inv[...] = jnp.sum(jnp.where(lane == row, inverse, 0.0), axis=0, keepdims=True)
    for index in order:
        pltpu.make_async_remote_copy(
            src_ref=own_inv, dst_ref=inv_in.at[patch],
            send_sem=send_sem.at[0], recv_sem=recv_sem.at[0], **to(after, FIRST + index),
        ).start()
    for piece in range(1, PIECES):
        pass_on(piece)

    @pl.when(jnp.logical_not(works))
    def _():
        for index in range(WORKERS):
            pl.semaphore_signal(ready_sem, inc=1, **to(section, FIRST + index))

    @pl.when(works)
    def _():
        flag_lane = lax.broadcasted_iota(jnp.int32, (tokens, patches), 1)
        flag_row = lax.broadcasted_iota(jnp.int32, (tokens, patches), 0)
        for load in loads:
            load.wait()
        fresh = jnp.sum(
            jnp.where(flag_lane == flag_row // tok_rows, flags[...].astype(jnp.float32), 0.0), axis=-1, keepdims=True
        ) > 0.5

        def prepare(numbers, states, inverse, number):
            modded = []
            for h, state in zip(numbers, states):
                here = slice(h * head, (h + 1) * head)
                modded.append(state * inverse * (1.0 + mod[1, number:number + 1, here]) + mod[0, number:number + 1, here])
            squared = [jnp.mean(rows * rows, axis=-1, keepdims=True) for rows in modded]
            ready = []
            for h, rows, square in zip(numbers, modded, squared):
                here = slice(h * head, (h + 1) * head)
                normed = rows * lax.rsqrt(square + epsilon)
                query = (normed * (qg[number:number + 1] * (1.0 / math.sqrt(head)))).astype(jnp.bfloat16)
                cached_k = cache_k[number, :, here].astype(jnp.float32)
                cached_v = cache_v[number, :, here].astype(jnp.float32)
                all_keys = jnp.where(fresh, normed * kg[number:number + 1], cached_k).astype(jnp.bfloat16)
                all_values = jnp.where(fresh, rows, cached_v).astype(jnp.bfloat16)
                ready.append((query, all_keys, all_values))
            return ready

        def attend(numbers, states, number, ready, first, last):
            scores = [
                lax.dot_general(
                    query[first:last], all_keys, (((1,), (1,)), ((), ())), preferred_element_type=jnp.float32
                )
                for query, all_keys, _ in ready
            ]
            largest = [jnp.max(score, axis=-1, keepdims=True) for score in scores]
            raised = [jnp.exp(score - most) for score, most in zip(scores, largest)]
            scale = [1.0 / jnp.sum(terms, axis=-1, keepdims=True) for terms in raised]
            weights = [(terms * one).astype(jnp.bfloat16) for terms, one in zip(raised, scale)]
            attended = [
                jnp.dot(weight, all_values, preferred_element_type=jnp.float32)
                for weight, (_, _, all_values) in zip(weights, ready)
            ]
            runs = count[...] > number
            updated = []
            for h, state, change in zip(numbers, states, attended):
                rows = state[first:last]
                moved = rows + mod[2, number:number + 1, h * head:(h + 1) * head] * change
                updated.append(jnp.where(runs, moved, rows))
            return updated

        pltpu.make_async_copy(inv_in, inv_in, recv_sem.at[0]).wait()
        spread = jnp.broadcast_to(inv_in[...], (patches, tok_rows, 128))
        inverse = jnp.sum(jnp.where((lane == row)[None], spread, 0.0), axis=-1, keepdims=True).reshape(tokens, 1)
        heads = part // head
        middle = []
        for piece in range(PIECES):
            arrived = state_in.at[:, pl.ds(piece * share, share)]
            pltpu.make_async_copy(arrived, arrived, recv_sem.at[4 + piece]).wait()
            numbers = range(piece * heads // PIECES, (piece + 1) * heads // PIECES)
            states = [state_in[:, h * head:(h + 1) * head].astype(jnp.float32) for h in numbers]
            middle += attend(numbers, states, 0, prepare(numbers, states, inverse, 0), 0, tokens)

        halves = tokens // 128
        lanes = lax.broadcasted_iota(jnp.int32, (128, 128), 1)
        diagonal = (lanes == lax.broadcasted_iota(jnp.int32, (128, 128), 0))[None]
        squares = functools.reduce(jnp.add, [state * state for state in middle])
        sums = jnp.sum(squares, axis=-1, keepdims=True).reshape(halves, 128, 1)
        own_sums[...] = jnp.sum(jnp.where(diagonal, sums, 0.0), axis=1)
        for step in range(1, WORKERS):
            pltpu.make_async_remote_copy(
                src_ref=own_sums, dst_ref=sums_in.at[slot], send_sem=send_sem.at[2], recv_sem=recv_sem.at[2],
                **to(section, FIRST + lax.rem(slot + step, WORKERS)),
            ).start()
        sums_in[slot] = own_sums[...]
        others = sums_in.at[pl.ds(0, WORKERS - 1)]
        pltpu.make_async_copy(others, others, recv_sem.at[2]).wait()
        total = lax.rsqrt(jnp.sum(sums_in[...], axis=0) * (1.0 / width) + epsilon)
        spread = jnp.broadcast_to(total[:, None, :], (halves, 128, 128))
        inverse = jnp.sum(jnp.where(diagonal, spread, 0.0), axis=-1, keepdims=True).reshape(tokens, 1)

        pl.semaphore_wait(ready_sem, patches - WORKERS)

        def give(partner, first, last):
            rows_there = pl.ds(partner * tok_rows, tok_rows)
            source = result.at[rows_there, pl.ds(first * head, (last - first) * head)]
            target = out.at[:, pl.ds(pl.multiple_of(mine * part + first * head, head), (last - first) * head)]

            def send():
                pltpu.make_async_remote_copy(
                    src_ref=source, dst_ref=target, send_sem=send_sem.at[3], recv_sem=recv_sem.at[3],
                    **to(section, partner),
                ).start()

            if FIRST <= partner < FIRST + WORKERS:
                pl.when(partner != patch)(send)

                @pl.when(partner == patch)
                def _():
                    pltpu.make_async_copy(source, target, load_sem.at[8]).start()
            else:
                send()

        numbers = range(heads)
        ready = prepare(numbers, middle, inverse, 1)
        for first, last, order in STEPS:
            for h, state in zip(numbers, attend(numbers, middle, 1, ready, first, last)):
                result[first:last, h * head:(h + 1) * head] = state.astype(result.dtype)
            for partner in order:
                give(partner, 0, heads)
        pltpu.make_async_copy(result.at[rows_here, :], out.at[:, column], load_sem.at[8]).wait()
        pltpu.make_async_copy(others, others, send_sem.at[2]).wait()
        rest = result.at[pl.ds(0, tokens - tok_rows), :]
        pltpu.make_async_copy(rest, rest, send_sem.at[3]).wait()
        arriving = out.at[:, pl.ds(0, width - part)]
        pltpu.make_async_copy(arriving, arriving, recv_sem.at[3]).wait()

    sent = inv_in.at[pl.ds(0, WORKERS)]
    pltpu.make_async_copy(sent, sent, send_sem.at[0]).wait()
    pltpu.make_async_copy(own_rows, own_rows, send_sem.at[1]).wait()

    @pl.when(jnp.logical_not(works))
    def _():
        pltpu.make_async_copy(out, out, recv_sem.at[3]).wait()


def per_device(previous, stale_keys, stale_values, modulation, q_gain, k_gain, blocks, refresh):
    sections = lax.axis_size("section")
    patches = lax.axis_size("patch")
    _, tok_rows, width = previous.shape
    _, layers, tokens, _ = stale_keys.shape
    head = q_gain.shape[-1]
    part = width // WORKERS
    anywhere = pl.BlockSpec(memory_space=pl.ANY)
    operands = (previous, stale_keys, stale_values, jnp.swapaxes(modulation, 1, 2), q_gain, k_gain, refresh)
    stay = [pltpu.with_memory_space_constraint(operand, pltpu.HBM) for operand in operands]
    mixed = pl.pallas_call(
        functools.partial(kernel, sections, patches, head),
        out_shape=pltpu.VMEM((tok_rows, width), jnp.bfloat16),
        in_specs=[anywhere] * 8,
        out_specs=pl.BlockSpec(memory_space=pltpu.VMEM),
        scratch_shapes=[
            pltpu.VMEM((tok_rows, width), jnp.bfloat16),
            pltpu.VMEM((1, 128), jnp.float32),
            pltpu.VMEM((tokens, part), jnp.bfloat16),
            pltpu.VMEM((patches, 1, 128), jnp.float32),
            pltpu.VMEM((layers, tokens, part), jnp.bfloat16),
            pltpu.VMEM((layers, tokens, part), jnp.bfloat16),
            pltpu.VMEM((3, layers, part), jnp.float32),
            pltpu.VMEM((layers, head), jnp.float32),
            pltpu.VMEM((layers, head), jnp.float32),
            pltpu.VMEM((1, patches), jnp.int32),
            pltpu.VMEM((1, 1), jnp.int32),
            pltpu.VMEM((tokens // 128, 128), jnp.float32),
            pltpu.VMEM((WORKERS, tokens // 128, 128), jnp.float32),
            pltpu.VMEM((tokens, part), jnp.bfloat16),
            pltpu.SemaphoreType.DMA((9,)),
            pltpu.SemaphoreType.DMA((4,)),
            pltpu.SemaphoreType.DMA((4 + PIECES,)),
            pltpu.SemaphoreType.REGULAR,
        ],
        compiler_params=pltpu.CompilerParams(
            collective_id=0, has_side_effects=True, vmem_limit_bytes=VMEM_BYTES
        ),
    )(*stay, blocks[None])
    return mixed.astype(jnp.float32)[None]


def solution(mesh):
    placed = (
        P("section", "patch", None),
        P("section", None, None, None),
        P("section", None, None, None),
        P("section", None, None, None),
        P("section", None, None),
        P("section", None, None),
        P("section"),
        P("section", None),
    )
    return jax.shard_map(
        per_device,
        mesh=mesh,
        in_specs=placed,
        out_specs=P("section", "patch", None),
        check_vma=False,
    )
```

```python
import functools
import math

import jax
import jax.numpy as jnp
from jax import lax
from jax.experimental import pallas as pl
from jax.experimental.pallas import tpu as pltpu
from jax.sharding import PartitionSpec as P

epsilon = 1e-06
VMEM_BYTES = 48 * 2**20
MESH = pl.DeviceIdType.MESH
PIECES = 2
STEPS = ((0, 128, (1, 3, 2, 0, 4, 5, 6, 7)), (128, 256, (14, 15, 8, 9, 12, 13, 10, 11)))
FIRST, WORKERS = 2, 4


def kernel(
    sections, patches, head, previous, stale_k, stale_v, modulation, q_gain, k_gain, refresh, blocks, out,
    own_rows, own_inv, state_in, inv_in, cache_k, cache_v, mod, qg, kg, flags, count,
    own_sums, sums_in, result, load_sem, send_sem, recv_sem, ready_sem,
):
    section = lax.axis_index("section")
    patch = lax.axis_index("patch")
    after = lax.rem(section + 1, sections)
    before = lax.rem(section + sections - 1, sections)
    tok_rows, width = own_rows.shape
    tokens, part = state_in.shape
    share = part // PIECES
    works = jnp.logical_and(patch >= FIRST, patch < FIRST + WORKERS)
    slot = lax.rem(patch + patches - FIRST, patches)
    mine = lax.rem(slot, WORKERS)
    column = pl.ds(pl.multiple_of(mine * part, part), part)
    rows_here = pl.ds(pl.multiple_of(patch * tok_rows, tok_rows), tok_rows)

    barrier = pltpu.get_barrier_semaphore()

    def to(where, partner):
        return {"device_id": {"section": where, "patch": partner}, "device_id_type": MESH}

    loads = [
        pltpu.make_async_copy(stale_k.at[0, :, :, column], cache_k, load_sem.at[1]),
        pltpu.make_async_copy(stale_v.at[0, :, :, column], cache_v, load_sem.at[2]),
        pltpu.make_async_copy(modulation.at[0, :, :, column], mod, load_sem.at[3]),
        pltpu.make_async_copy(q_gain.at[0], qg, load_sem.at[4]),
        pltpu.make_async_copy(k_gain.at[0], kg, load_sem.at[5]),
        pltpu.make_async_copy(refresh, flags, load_sem.at[6]),
        pltpu.make_async_copy(blocks, count, load_sem.at[7]),
    ]
    load_rows = pltpu.make_async_copy(previous.at[0], own_rows, load_sem.at[0])

    @pl.when(works)
    def _():
        for partner in range(patches - 1, -1, -1):
            pl.semaphore_signal(barrier, inc=1, **to(before, partner))
        for partner in range(patches - 1, -1, -1):
            @pl.when(partner != patch)
            def _():
                pl.semaphore_signal(barrier, inc=1, **to(section, partner))
        for load in loads:
            load.start()

    pl.semaphore_wait(barrier, 2 * WORKERS - works.astype(jnp.int32))

    order = range(WORKERS - 1, -1, -1)

    def pass_on(piece):
        for index in order:
            begin = pl.multiple_of(index * part + piece * share, share)
            pltpu.make_async_remote_copy(
                src_ref=previous.at[0, :, pl.ds(begin, share)],
                dst_ref=state_in.at[rows_here, pl.ds(piece * share, share)],
                send_sem=send_sem.at[1], recv_sem=recv_sem.at[4 + piece], **to(after, FIRST + index),
            ).start()

    pass_on(0)
    load_rows.start()
    load_rows.wait()
    rows = own_rows[...].astype(jnp.float32)
    lane = lax.broadcasted_iota(jnp.int32, (tok_rows, 128), 1)
    row = lax.broadcasted_iota(jnp.int32, (tok_rows, 128), 0)
    inverse = lax.rsqrt(jnp.mean(rows * rows, axis=-1, keepdims=True) + epsilon)
    own_inv[...] = jnp.sum(jnp.where(lane == row, inverse, 0.0), axis=0, keepdims=True)
    for index in order:
        pltpu.make_async_remote_copy(
            src_ref=own_inv, dst_ref=inv_in.at[patch],
            send_sem=send_sem.at[0], recv_sem=recv_sem.at[0], **to(after, FIRST + index),
        ).start()
    for piece in range(1, PIECES):
        pass_on(piece)

    @pl.when(jnp.logical_not(works))
    def _():
        for index in range(WORKERS):
            pl.semaphore_signal(ready_sem, inc=1, **to(section, FIRST + index))

    @pl.when(works)
    def _():
        flag_lane = lax.broadcasted_iota(jnp.int32, (tokens, patches), 1)
        flag_row = lax.broadcasted_iota(jnp.int32, (tokens, patches), 0)
        for load in loads:
            load.wait()
        fresh = jnp.sum(
            jnp.where(flag_lane == flag_row // tok_rows, flags[...].astype(jnp.float32), 0.0), axis=-1, keepdims=True
        )
        fresh = jnp.broadcast_to(fresh, (tokens, head)).astype(jnp.bfloat16) > 0.5

        def prepare(numbers, states, inverse, number):
            modded = []
            for h, state in zip(numbers, states):
                here = slice(h * head, (h + 1) * head)
                modded.append(state * inverse * (1.0 + mod[1, number:number + 1, here]) + mod[0, number:number + 1, here])
            squared = [jnp.mean(rows * rows, axis=-1, keepdims=True) for rows in modded]
            ready = []
            for h, rows, square in zip(numbers, modded, squared):
                here = slice(h * head, (h + 1) * head)
                normed = rows * lax.rsqrt(square + epsilon)
                query = (normed * (qg[number:number + 1] * (1.0 / math.sqrt(head)))).astype(jnp.bfloat16)
                fresh_k = (normed * kg[number:number + 1]).astype(jnp.bfloat16)
                all_keys = jnp.where(fresh, fresh_k, cache_k[number, :, here])
                all_values = jnp.where(fresh, rows.astype(jnp.bfloat16), cache_v[number, :, here])
                ready.append((query, all_keys, all_values))
            return ready

        def attend(numbers, states, number, ready, first, last):
            scores = [
                lax.dot_general(
                    query[first:last], all_keys, (((1,), (1,)), ((), ())), preferred_element_type=jnp.float32
                )
                for query, all_keys, _ in ready
            ]
            largest = [jnp.max(score, axis=-1, keepdims=True) for score in scores]
            raised = [jnp.exp(score - most) for score, most in zip(scores, largest)]
            scale = [1.0 / jnp.sum(terms, axis=-1, keepdims=True) for terms in raised]
            weights = [(terms * one).astype(jnp.bfloat16) for terms, one in zip(raised, scale)]
            attended = [
                jnp.dot(weight, all_values, preferred_element_type=jnp.float32)
                for weight, (_, _, all_values) in zip(weights, ready)
            ]
            runs = count[...] > number
            updated = []
            for h, state, change in zip(numbers, states, attended):
                rows = state[first:last]
                moved = rows + mod[2, number:number + 1, h * head:(h + 1) * head] * change
                updated.append(jnp.where(runs, moved, rows))
            return updated

        pltpu.make_async_copy(inv_in, inv_in, recv_sem.at[0]).wait()
        spread = jnp.broadcast_to(inv_in[...], (patches, tok_rows, 128))
        inverse = jnp.sum(jnp.where((lane == row)[None], spread, 0.0), axis=-1, keepdims=True).reshape(tokens, 1)
        heads = part // head
        middle = []
        for piece in range(PIECES):
            arrived = state_in.at[:, pl.ds(piece * share, share)]
            pltpu.make_async_copy(arrived, arrived, recv_sem.at[4 + piece]).wait()
        states = [state_in[:, h * head:(h + 1) * head].astype(jnp.float32) for h in range(heads)]
        middle = attend(range(heads), states, 0, prepare(range(heads), states, inverse, 0), 0, tokens)

        halves = tokens // 128
        lanes = lax.broadcasted_iota(jnp.int32, (128, 128), 1)
        diagonal = (lanes == lax.broadcasted_iota(jnp.int32, (128, 128), 0))[None]
        squares = functools.reduce(jnp.add, [state * state for state in middle])
        sums = jnp.sum(squares, axis=-1, keepdims=True).reshape(halves, 128, 1)
        own_sums[...] = jnp.sum(jnp.where(diagonal, sums, 0.0), axis=1)
        for step in range(1, WORKERS):
            pltpu.make_async_remote_copy(
                src_ref=own_sums, dst_ref=sums_in.at[slot], send_sem=send_sem.at[2], recv_sem=recv_sem.at[2],
                **to(section, FIRST + lax.rem(slot + step, WORKERS)),
            ).start()
        sums_in[slot] = own_sums[...]
        others = sums_in.at[pl.ds(0, WORKERS - 1)]
        pltpu.make_async_copy(others, others, recv_sem.at[2]).wait()
        total = lax.rsqrt(jnp.sum(sums_in[...], axis=0) * (1.0 / width) + epsilon)
        spread = jnp.broadcast_to(total[:, None, :], (halves, 128, 128))
        inverse = jnp.sum(jnp.where(diagonal, spread, 0.0), axis=-1, keepdims=True).reshape(tokens, 1)

        pl.semaphore_wait(ready_sem, patches - WORKERS)

        def give(partner, first, last):
            rows_there = pl.ds(partner * tok_rows, tok_rows)
            source = result.at[rows_there, pl.ds(first * head, (last - first) * head)]
            target = out.at[:, pl.ds(pl.multiple_of(mine * part + first * head, head), (last - first) * head)]

            def send():
                pltpu.make_async_remote_copy(
                    src_ref=source, dst_ref=target, send_sem=send_sem.at[3], recv_sem=recv_sem.at[3],
                    **to(section, partner),
                ).start()

            if FIRST <= partner < FIRST + WORKERS:
                pl.when(partner != patch)(send)

                @pl.when(partner == patch)
                def _():
                    pltpu.make_async_copy(source, target, load_sem.at[8]).start()
            else:
                send()

        numbers = range(heads)
        ready = prepare(numbers, middle, inverse, 1)
        for first, last, order in STEPS:
            for h, state in zip(numbers, attend(numbers, middle, 1, ready, first, last)):
                result[first:last, h * head:(h + 1) * head] = state.astype(result.dtype)
            for partner in order:
                give(partner, 0, heads)
        pltpu.make_async_copy(result.at[rows_here, :], out.at[:, column], load_sem.at[8]).wait()
        pltpu.make_async_copy(others, others, send_sem.at[2]).wait()
        rest = result.at[pl.ds(0, tokens - tok_rows), :]
        pltpu.make_async_copy(rest, rest, send_sem.at[3]).wait()
        arriving = out.at[:, pl.ds(0, width - part)]
        pltpu.make_async_copy(arriving, arriving, recv_sem.at[3]).wait()

    sent = inv_in.at[pl.ds(0, WORKERS)]
    pltpu.make_async_copy(sent, sent, send_sem.at[0]).wait()
    pltpu.make_async_copy(own_rows, own_rows, send_sem.at[1]).wait()

    @pl.when(jnp.logical_not(works))
    def _():
        pltpu.make_async_copy(out, out, recv_sem.at[3]).wait()


def per_device(previous, stale_keys, stale_values, modulation, q_gain, k_gain, blocks, refresh):
    sections = lax.axis_size("section")
    patches = lax.axis_size("patch")
    _, tok_rows, width = previous.shape
    _, layers, tokens, _ = stale_keys.shape
    head = q_gain.shape[-1]
    part = width // WORKERS
    anywhere = pl.BlockSpec(memory_space=pl.ANY)
    operands = (previous, stale_keys, stale_values, jnp.swapaxes(modulation, 1, 2), q_gain, k_gain, refresh)
    stay = [pltpu.with_memory_space_constraint(operand, pltpu.HBM) for operand in operands]
    mixed = pl.pallas_call(
        functools.partial(kernel, sections, patches, head),
        out_shape=pltpu.VMEM((tok_rows, width), jnp.bfloat16),
        in_specs=[anywhere] * 8,
        out_specs=pl.BlockSpec(memory_space=pltpu.VMEM),
        scratch_shapes=[
            pltpu.VMEM((tok_rows, width), jnp.bfloat16),
            pltpu.VMEM((1, 128), jnp.float32),
            pltpu.VMEM((tokens, part), jnp.bfloat16),
            pltpu.VMEM((patches, 1, 128), jnp.float32),
            pltpu.VMEM((layers, tokens, part), jnp.bfloat16),
            pltpu.VMEM((layers, tokens, part), jnp.bfloat16),
            pltpu.VMEM((3, layers, part), jnp.float32),
            pltpu.VMEM((layers, head), jnp.float32),
            pltpu.VMEM((layers, head), jnp.float32),
            pltpu.VMEM((1, patches), jnp.int32),
            pltpu.VMEM((1, 1), jnp.int32),
            pltpu.VMEM((tokens // 128, 128), jnp.float32),
            pltpu.VMEM((WORKERS, tokens // 128, 128), jnp.float32),
            pltpu.VMEM((tokens, part), jnp.bfloat16),
            pltpu.SemaphoreType.DMA((9,)),
            pltpu.SemaphoreType.DMA((4,)),
            pltpu.SemaphoreType.DMA((4 + PIECES,)),
            pltpu.SemaphoreType.REGULAR,
        ],
        compiler_params=pltpu.CompilerParams(
            collective_id=0, has_side_effects=True, vmem_limit_bytes=VMEM_BYTES
        ),
    )(*stay, blocks[None])
    return mixed.astype(jnp.float32)[None]


def solution(mesh):
    placed = (
        P("section", "patch", None),
        P("section", None, None, None),
        P("section", None, None, None),
        P("section", None, None, None),
        P("section", None, None),
        P("section", None, None),
        P("section"),
        P("section", None),
    )
    return jax.shard_map(
        per_device,
        mesh=mesh,
        in_specs=placed,
        out_specs=P("section", "patch", None),
        check_vma=False,
    )
```

```python
import functools
import math

import jax
import jax.numpy as jnp
from jax import lax
from jax.experimental import pallas as pl
from jax.experimental.pallas import tpu as pltpu
from jax.sharding import PartitionSpec as P

epsilon = 1e-06
VMEM_BYTES = 48 * 2**20
MESH = pl.DeviceIdType.MESH
PIECES = 2
STEPS = ((0, 128, (1, 3, 2, 0, 4, 5, 6, 7)), (128, 256, (14, 15, 8, 9, 12, 13, 10, 11)))
FIRST, WORKERS = 2, 4


def kernel(
    sections, patches, head, previous, stale_k, stale_v, modulation, q_gain, k_gain, refresh, blocks, out,
    own_rows, own_inv, state_in, inv_in, cache_k, cache_v, mod, qg, kg, flags, count,
    own_sums, sums_in, result, load_sem, send_sem, recv_sem, ready_sem,
):
    section = lax.axis_index("section")
    patch = lax.axis_index("patch")
    after = lax.rem(section + 1, sections)
    before = lax.rem(section + sections - 1, sections)
    tok_rows, width = own_rows.shape
    tokens, part = state_in.shape
    share = part // PIECES
    works = jnp.logical_and(patch >= FIRST, patch < FIRST + WORKERS)
    slot = lax.rem(patch + patches - FIRST, patches)
    mine = lax.rem(slot, WORKERS)
    column = pl.ds(pl.multiple_of(mine * part, part), part)
    rows_here = pl.ds(pl.multiple_of(patch * tok_rows, tok_rows), tok_rows)

    barrier = pltpu.get_barrier_semaphore()

    def to(where, partner):
        return {"device_id": {"section": where, "patch": partner}, "device_id_type": MESH}

    loads = [
        pltpu.make_async_copy(stale_k.at[0, :, :, column], cache_k, load_sem.at[1]),
        pltpu.make_async_copy(stale_v.at[0, :, :, column], cache_v, load_sem.at[2]),
        pltpu.make_async_copy(modulation.at[0, :, :, column], mod, load_sem.at[3]),
        pltpu.make_async_copy(q_gain.at[0], qg, load_sem.at[4]),
        pltpu.make_async_copy(k_gain.at[0], kg, load_sem.at[5]),
        pltpu.make_async_copy(refresh, flags, load_sem.at[6]),
        pltpu.make_async_copy(blocks, count, load_sem.at[7]),
    ]
    load_rows = pltpu.make_async_copy(previous.at[0], own_rows, load_sem.at[0])

    @pl.when(works)
    def _():
        for partner in range(patches - 1, -1, -1):
            pl.semaphore_signal(barrier, inc=1, **to(before, partner))
        for load in loads:
            load.start()

    pl.semaphore_wait(barrier, WORKERS)

    order = range(WORKERS - 1, -1, -1)

    def pass_on(piece):
        for index in order:
            begin = pl.multiple_of(index * part + piece * share, share)
            pltpu.make_async_remote_copy(
                src_ref=previous.at[0, :, pl.ds(begin, share)],
                dst_ref=state_in.at[rows_here, pl.ds(piece * share, share)],
                send_sem=send_sem.at[1], recv_sem=recv_sem.at[4 + piece], **to(after, FIRST + index),
            ).start()

    pass_on(0)
    load_rows.start()
    load_rows.wait()
    rows = own_rows[...].astype(jnp.float32)
    lane = lax.broadcasted_iota(jnp.int32, (tok_rows, 128), 1)
    row = lax.broadcasted_iota(jnp.int32, (tok_rows, 128), 0)
    inverse = lax.rsqrt(jnp.mean(rows * rows, axis=-1, keepdims=True) + epsilon)
    own_inv[...] = jnp.sum(jnp.where(lane == row, inverse, 0.0), axis=0, keepdims=True)
    for index in order:
        pltpu.make_async_remote_copy(
            src_ref=own_inv, dst_ref=inv_in.at[patch],
            send_sem=send_sem.at[0], recv_sem=recv_sem.at[0], **to(after, FIRST + index),
        ).start()
    for piece in range(1, PIECES):
        pass_on(piece)

    @pl.when(works)
    def _():
        flag_lane = lax.broadcasted_iota(jnp.int32, (tokens, patches), 1)
        flag_row = lax.broadcasted_iota(jnp.int32, (tokens, patches), 0)
        for load in loads:
            load.wait()
        fresh = jnp.sum(
            jnp.where(flag_lane == flag_row // tok_rows, flags[...].astype(jnp.float32), 0.0), axis=-1, keepdims=True
        )
        fresh = jnp.broadcast_to(fresh, (tokens, head)).astype(jnp.bfloat16) > 0.5

        def prepare(numbers, states, inverse, number):
            modded = []
            for h, state in zip(numbers, states):
                here = slice(h * head, (h + 1) * head)
                modded.append(state * inverse * (1.0 + mod[1, number:number + 1, here]) + mod[0, number:number + 1, here])
            squared = [jnp.mean(rows * rows, axis=-1, keepdims=True) for rows in modded]
            ready = []
            for h, rows, square in zip(numbers, modded, squared):
                here = slice(h * head, (h + 1) * head)
                normed = rows * lax.rsqrt(square + epsilon)
                query = (normed * (qg[number:number + 1] * (1.0 / math.sqrt(head)))).astype(jnp.bfloat16)
                fresh_k = (normed * kg[number:number + 1]).astype(jnp.bfloat16)
                all_keys = jnp.where(fresh, fresh_k, cache_k[number, :, here])
                all_values = jnp.where(fresh, rows.astype(jnp.bfloat16), cache_v[number, :, here])
                ready.append((query, all_keys, all_values))
            return ready

        def attend(numbers, states, number, ready, first, last):
            scores = [
                lax.dot_general(
                    query[first:last], all_keys, (((1,), (1,)), ((), ())), preferred_element_type=jnp.float32
                )
                for query, all_keys, _ in ready
            ]
            largest = [jnp.max(score, axis=-1, keepdims=True) for score in scores]
            raised = [jnp.exp(score - most) for score, most in zip(scores, largest)]
            scale = [1.0 / jnp.sum(terms, axis=-1, keepdims=True) for terms in raised]
            weights = [(terms * one).astype(jnp.bfloat16) for terms, one in zip(raised, scale)]
            attended = [
                jnp.dot(weight, all_values, preferred_element_type=jnp.float32)
                for weight, (_, _, all_values) in zip(weights, ready)
            ]
            runs = count[...] > number
            updated = []
            for h, state, change in zip(numbers, states, attended):
                rows = state[first:last]
                moved = rows + mod[2, number:number + 1, h * head:(h + 1) * head] * change
                updated.append(jnp.where(runs, moved, rows))
            return updated

        pltpu.make_async_copy(inv_in, inv_in, recv_sem.at[0]).wait()
        spread = jnp.broadcast_to(inv_in[...], (patches, tok_rows, 128))
        inverse = jnp.sum(jnp.where((lane == row)[None], spread, 0.0), axis=-1, keepdims=True).reshape(tokens, 1)
        heads = part // head
        middle = []
        for piece in range(PIECES):
            arrived = state_in.at[:, pl.ds(piece * share, share)]
            pltpu.make_async_copy(arrived, arrived, recv_sem.at[4 + piece]).wait()
        pl.semaphore_signal(ready_sem, inc=1, **to(before, patch))
        states = [state_in[:, h * head:(h + 1) * head].astype(jnp.float32) for h in range(heads)]
        middle = attend(range(heads), states, 0, prepare(range(heads), states, inverse, 0), 0, tokens)

        halves = tokens // 128
        lanes = lax.broadcasted_iota(jnp.int32, (128, 128), 1)
        diagonal = (lanes == lax.broadcasted_iota(jnp.int32, (128, 128), 0))[None]
        squares = functools.reduce(jnp.add, [state * state for state in middle])
        sums = jnp.sum(squares, axis=-1, keepdims=True).reshape(halves, 128, 1)
        own_sums[...] = jnp.sum(jnp.where(diagonal, sums, 0.0), axis=1)
        for step in range(1, WORKERS):
            pltpu.make_async_remote_copy(
                src_ref=own_sums, dst_ref=sums_in.at[slot], send_sem=send_sem.at[2], recv_sem=recv_sem.at[2],
                **to(section, FIRST + lax.rem(slot + step, WORKERS)),
            ).start()
        sums_in[slot] = own_sums[...]
        others = sums_in.at[pl.ds(0, WORKERS - 1)]
        pltpu.make_async_copy(others, others, recv_sem.at[2]).wait()
        total = lax.rsqrt(jnp.sum(sums_in[...], axis=0) * (1.0 / width) + epsilon)
        spread = jnp.broadcast_to(total[:, None, :], (halves, 128, 128))
        inverse = jnp.sum(jnp.where(diagonal, spread, 0.0), axis=-1, keepdims=True).reshape(tokens, 1)

        pl.semaphore_wait(ready_sem, 1)

        def give(partner, first, last):
            rows_there = pl.ds(partner * tok_rows, tok_rows)
            source = result.at[rows_there, pl.ds(first * head, (last - first) * head)]
            target = out.at[:, pl.ds(pl.multiple_of(mine * part + first * head, head), (last - first) * head)]

            def send():
                pltpu.make_async_remote_copy(
                    src_ref=source, dst_ref=target, send_sem=send_sem.at[3], recv_sem=recv_sem.at[3],
                    **to(section, partner),
                ).start()

            if FIRST <= partner < FIRST + WORKERS:
                pl.when(partner != patch)(send)

                @pl.when(partner == patch)
                def _():
                    pltpu.make_async_copy(source, target, load_sem.at[8]).start()
            else:
                send()

        numbers = range(heads)
        ready = prepare(numbers, middle, inverse, 1)
        for first, last, order in STEPS:
            for h, state in zip(numbers, attend(numbers, middle, 1, ready, first, last)):
                result[first:last, h * head:(h + 1) * head] = state.astype(result.dtype)
            for partner in order:
                give(partner, 0, heads)
        pltpu.make_async_copy(result.at[rows_here, :], out.at[:, column], load_sem.at[8]).wait()
        pltpu.make_async_copy(others, others, send_sem.at[2]).wait()
        rest = result.at[pl.ds(0, tokens - tok_rows), :]
        pltpu.make_async_copy(rest, rest, send_sem.at[3]).wait()
        arriving = out.at[:, pl.ds(0, width - part)]
        pltpu.make_async_copy(arriving, arriving, recv_sem.at[3]).wait()

    sent = inv_in.at[pl.ds(0, WORKERS)]
    pltpu.make_async_copy(sent, sent, send_sem.at[0]).wait()
    pltpu.make_async_copy(own_rows, own_rows, send_sem.at[1]).wait()

    @pl.when(jnp.logical_not(works))
    def _():
        pltpu.make_async_copy(out, out, recv_sem.at[3]).wait()


def per_device(previous, stale_keys, stale_values, modulation, q_gain, k_gain, blocks, refresh):
    sections = lax.axis_size("section")
    patches = lax.axis_size("patch")
    _, tok_rows, width = previous.shape
    _, layers, tokens, _ = stale_keys.shape
    head = q_gain.shape[-1]
    part = width // WORKERS
    anywhere = pl.BlockSpec(memory_space=pl.ANY)
    operands = (previous, stale_keys, stale_values, jnp.swapaxes(modulation, 1, 2), q_gain, k_gain, refresh)
    stay = [pltpu.with_memory_space_constraint(operand, pltpu.HBM) for operand in operands]
    mixed = pl.pallas_call(
        functools.partial(kernel, sections, patches, head),
        out_shape=pltpu.VMEM((tok_rows, width), jnp.bfloat16),
        in_specs=[anywhere] * 8,
        out_specs=pl.BlockSpec(memory_space=pltpu.VMEM),
        scratch_shapes=[
            pltpu.VMEM((tok_rows, width), jnp.bfloat16),
            pltpu.VMEM((1, 128), jnp.float32),
            pltpu.VMEM((tokens, part), jnp.bfloat16),
            pltpu.VMEM((patches, 1, 128), jnp.float32),
            pltpu.VMEM((layers, tokens, part), jnp.bfloat16),
            pltpu.VMEM((layers, tokens, part), jnp.bfloat16),
            pltpu.VMEM((3, layers, part), jnp.float32),
            pltpu.VMEM((layers, head), jnp.float32),
            pltpu.VMEM((layers, head), jnp.float32),
            pltpu.VMEM((1, patches), jnp.int32),
            pltpu.VMEM((1, 1), jnp.int32),
            pltpu.VMEM((tokens // 128, 128), jnp.float32),
            pltpu.VMEM((WORKERS, tokens // 128, 128), jnp.float32),
            pltpu.VMEM((tokens, part), jnp.bfloat16),
            pltpu.SemaphoreType.DMA((9,)),
            pltpu.SemaphoreType.DMA((4,)),
            pltpu.SemaphoreType.DMA((4 + PIECES,)),
            pltpu.SemaphoreType.REGULAR,
        ],
        compiler_params=pltpu.CompilerParams(
            collective_id=0, has_side_effects=True, vmem_limit_bytes=VMEM_BYTES
        ),
    )(*stay, blocks[None])
    return mixed.astype(jnp.float32)[None]


def solution(mesh):
    placed = (
        P("section", "patch", None),
        P("section", None, None, None),
        P("section", None, None, None),
        P("section", None, None, None),
        P("section", None, None),
        P("section", None, None),
        P("section"),
        P("section", None),
    )
    return jax.shard_map(
        per_device,
        mesh=mesh,
        in_specs=placed,
        out_specs=P("section", "patch", None),
        check_vma=False,
    )
```

```python
import functools
import math

import jax
import jax.numpy as jnp
from jax import lax
from jax.experimental import pallas as pl
from jax.experimental.pallas import tpu as pltpu
from jax.sharding import PartitionSpec as P

epsilon = 1e-06
VMEM_BYTES = 48 * 2**20
MESH = pl.DeviceIdType.MESH
PIECES = 2
STEPS = ((0, 128, (1, 3, 2, 0, 4, 5, 6, 7)), (128, 256, (14, 15, 8, 9, 12, 13, 10, 11)))
FIRST, WORKERS = 2, 4


def kernel(
    sections, patches, head, previous, stale_k, stale_v, modulation, q_gain, k_gain, refresh, blocks, out,
    own_rows, own_inv, state_in, inv_in, cache_k, cache_v, mod, qg, kg, flags, count,
    own_sums, sums_in, result, load_sem, send_sem, recv_sem, ready_sem,
):
    section = lax.axis_index("section")
    patch = lax.axis_index("patch")
    after = lax.rem(section + 1, sections)
    before = lax.rem(section + sections - 1, sections)
    tok_rows, width = own_rows.shape
    tokens, part = state_in.shape
    share = part // PIECES
    layers = cache_k.shape[0]
    works = jnp.logical_and(patch >= FIRST, patch < FIRST + WORKERS)
    slot = lax.rem(patch + patches - FIRST, patches)
    mine = lax.rem(slot, WORKERS)
    column = pl.ds(pl.multiple_of(mine * part, part), part)
    rows_here = pl.ds(pl.multiple_of(patch * tok_rows, tok_rows), tok_rows)

    barrier = pltpu.get_barrier_semaphore()

    def to(where, partner):
        return {"device_id": {"section": where, "patch": partner}, "device_id_type": MESH}

    loads = [
        pltpu.make_async_copy(stale_k.at[0, :, :, column], cache_k, load_sem.at[1]),
        pltpu.make_async_copy(stale_v.at[0, :, :, column], cache_v, load_sem.at[2]),
        pltpu.make_async_copy(modulation.at[0, :, :, column], mod, load_sem.at[3]),
        pltpu.make_async_copy(q_gain.at[0], qg, load_sem.at[4]),
        pltpu.make_async_copy(k_gain.at[0], kg, load_sem.at[5]),
        pltpu.make_async_copy(refresh, flags, load_sem.at[6]),
        pltpu.make_async_copy(blocks, count, load_sem.at[7]),
    ]
    load_rows = pltpu.make_async_copy(previous.at[0], own_rows, load_sem.at[0])

    @pl.when(works)
    def _():
        for partner in range(patches - 1, -1, -1):
            pl.semaphore_signal(barrier, inc=1, **to(before, partner))
        for partner in range(patches - 1, -1, -1):
            @pl.when(partner != patch)
            def _():
                pl.semaphore_signal(barrier, inc=1, **to(section, partner))
        for load in loads:
            load.start()

    pl.semaphore_wait(barrier, 2 * WORKERS - works.astype(jnp.int32))

    order = range(WORKERS - 1, -1, -1)

    def pass_on(piece):
        for index in order:
            begin = pl.multiple_of(index * part + piece * share, share)
            pltpu.make_async_remote_copy(
                src_ref=previous.at[0, :, pl.ds(begin, share)],
                dst_ref=state_in.at[rows_here, pl.ds(piece * share, share)],
                send_sem=send_sem.at[1], recv_sem=recv_sem.at[4 + piece], **to(after, FIRST + index),
            ).start()

    pass_on(0)
    load_rows.start()
    load_rows.wait()
    rows = own_rows[...].astype(jnp.float32)
    lane = lax.broadcasted_iota(jnp.int32, (tok_rows, 128), 1)
    row = lax.broadcasted_iota(jnp.int32, (tok_rows, 128), 0)
    inverse = lax.rsqrt(jnp.mean(rows * rows, axis=-1, keepdims=True) + epsilon)
    own_inv[...] = jnp.sum(jnp.where(lane == row, inverse, 0.0), axis=0, keepdims=True)
    for index in order:
        pltpu.make_async_remote_copy(
            src_ref=own_inv, dst_ref=inv_in.at[patch],
            send_sem=send_sem.at[0], recv_sem=recv_sem.at[0], **to(after, FIRST + index),
        ).start()
    for piece in range(1, PIECES):
        pass_on(piece)

    @pl.when(jnp.logical_not(works))
    def _():
        for index in range(WORKERS):
            pl.semaphore_signal(ready_sem, inc=1, **to(section, FIRST + index))

    @pl.when(works)
    def _():
        flag_lane = lax.broadcasted_iota(jnp.int32, (tokens, patches), 1)
        flag_row = lax.broadcasted_iota(jnp.int32, (tokens, patches), 0)
        for load in loads:
            load.wait()
        fresh = jnp.sum(
            jnp.where(flag_lane == flag_row // tok_rows, flags[...].astype(jnp.float32), 0.0), axis=-1, keepdims=True
        )
        fresh = jnp.broadcast_to(fresh, (tokens, head)).astype(jnp.bfloat16) > 0.5

        def prepare(numbers, states, inverse, number):
            modded = []
            for h, state in zip(numbers, states):
                here = slice(h * head, (h + 1) * head)
                modded.append(state * inverse * (1.0 + mod[1, number:number + 1, here]) + mod[0, number:number + 1, here])
            squared = [jnp.mean(rows * rows, axis=-1, keepdims=True) for rows in modded]
            ready = []
            for h, rows, square in zip(numbers, modded, squared):
                here = slice(h * head, (h + 1) * head)
                normed = rows * lax.rsqrt(square + epsilon)
                query = (normed * (qg[number:number + 1] * (1.0 / math.sqrt(head)))).astype(jnp.bfloat16)
                fresh_k = (normed * kg[number:number + 1]).astype(jnp.bfloat16)
                all_keys = jnp.where(fresh, fresh_k, cache_k[number, :, here])
                all_values = jnp.where(fresh, rows.astype(jnp.bfloat16), cache_v[number, :, here])
                ready.append((query, all_keys, all_values))
            return ready

        def attend(numbers, states, number, ready, first, last):
            scores = [
                lax.dot_general(
                    query[first:last], all_keys, (((1,), (1,)), ((), ())), preferred_element_type=jnp.float32
                )
                for query, all_keys, _ in ready
            ]
            largest = [jnp.max(score, axis=-1, keepdims=True) for score in scores]
            raised = [jnp.exp(score - most) for score, most in zip(scores, largest)]
            if number == layers - 1:
                product = [
                    jnp.dot(
                        terms.astype(jnp.bfloat16),
                        jnp.concatenate([all_values, jnp.ones_like(all_values)], axis=1),
                        preferred_element_type=jnp.float32,
                    )
                    for terms, (_, _, all_values) in zip(raised, ready)
                ]
                attended = [both[:, :head] / both[:, head:] for both in product]
                return settle(numbers, states, number, attended, first, last)
            scale = [1.0 / jnp.sum(terms, axis=-1, keepdims=True) for terms in raised]
            weights = [(terms * one).astype(jnp.bfloat16) for terms, one in zip(raised, scale)]
            attended = [
                jnp.dot(weight, all_values, preferred_element_type=jnp.float32)
                for weight, (_, _, all_values) in zip(weights, ready)
            ]
            return settle(numbers, states, number, attended, first, last)

        def settle(numbers, states, number, attended, first, last):
            runs = count[...] > number
            updated = []
            for h, state, change in zip(numbers, states, attended):
                rows = state[first:last]
                moved = rows + mod[2, number:number + 1, h * head:(h + 1) * head] * change
                updated.append(jnp.where(runs, moved, rows))
            return updated

        pltpu.make_async_copy(inv_in, inv_in, recv_sem.at[0]).wait()
        spread = jnp.broadcast_to(inv_in[...], (patches, tok_rows, 128))
        inverse = jnp.sum(jnp.where((lane == row)[None], spread, 0.0), axis=-1, keepdims=True).reshape(tokens, 1)
        heads = part // head
        middle = []
        for piece in range(PIECES):
            arrived = state_in.at[:, pl.ds(piece * share, share)]
            pltpu.make_async_copy(arrived, arrived, recv_sem.at[4 + piece]).wait()
        states = [state_in[:, h * head:(h + 1) * head].astype(jnp.float32) for h in range(heads)]
        middle = attend(range(heads), states, 0, prepare(range(heads), states, inverse, 0), 0, tokens)

        halves = tokens // 128
        lanes = lax.broadcasted_iota(jnp.int32, (128, 128), 1)
        diagonal = (lanes == lax.broadcasted_iota(jnp.int32, (128, 128), 0))[None]
        squares = functools.reduce(jnp.add, [state * state for state in middle])
        sums = jnp.sum(squares, axis=-1, keepdims=True).reshape(halves, 128, 1)
        own_sums[...] = jnp.sum(jnp.where(diagonal, sums, 0.0), axis=1)
        for step in range(1, WORKERS):
            pltpu.make_async_remote_copy(
                src_ref=own_sums, dst_ref=sums_in.at[slot], send_sem=send_sem.at[2], recv_sem=recv_sem.at[2],
                **to(section, FIRST + lax.rem(slot + step, WORKERS)),
            ).start()
        sums_in[slot] = own_sums[...]
        others = sums_in.at[pl.ds(0, WORKERS - 1)]
        pltpu.make_async_copy(others, others, recv_sem.at[2]).wait()
        total = lax.rsqrt(jnp.sum(sums_in[...], axis=0) * (1.0 / width) + epsilon)
        spread = jnp.broadcast_to(total[:, None, :], (halves, 128, 128))
        inverse = jnp.sum(jnp.where(diagonal, spread, 0.0), axis=-1, keepdims=True).reshape(tokens, 1)

        pl.semaphore_wait(ready_sem, patches - WORKERS)

        def give(partner, first, last):
            rows_there = pl.ds(partner * tok_rows, tok_rows)
            source = result.at[rows_there, pl.ds(first * head, (last - first) * head)]
            target = out.at[:, pl.ds(pl.multiple_of(mine * part + first * head, head), (last - first) * head)]

            def send():
                pltpu.make_async_remote_copy(
                    src_ref=source, dst_ref=target, send_sem=send_sem.at[3], recv_sem=recv_sem.at[3],
                    **to(section, partner),
                ).start()

            if FIRST <= partner < FIRST + WORKERS:
                pl.when(partner != patch)(send)

                @pl.when(partner == patch)
                def _():
                    pltpu.make_async_copy(source, target, load_sem.at[8]).start()
            else:
                send()

        numbers = range(heads)
        ready = prepare(numbers, middle, inverse, 1)
        for first, last, order in STEPS:
            for h, state in zip(numbers, attend(numbers, middle, 1, ready, first, last)):
                result[first:last, h * head:(h + 1) * head] = state.astype(result.dtype)
            for partner in order:
                give(partner, 0, heads)
        pltpu.make_async_copy(result.at[rows_here, :], out.at[:, column], load_sem.at[8]).wait()
        pltpu.make_async_copy(others, others, send_sem.at[2]).wait()
        rest = result.at[pl.ds(0, tokens - tok_rows), :]
        pltpu.make_async_copy(rest, rest, send_sem.at[3]).wait()
        arriving = out.at[:, pl.ds(0, width - part)]
        pltpu.make_async_copy(arriving, arriving, recv_sem.at[3]).wait()

    sent = inv_in.at[pl.ds(0, WORKERS)]
    pltpu.make_async_copy(sent, sent, send_sem.at[0]).wait()
    pltpu.make_async_copy(own_rows, own_rows, send_sem.at[1]).wait()

    @pl.when(jnp.logical_not(works))
    def _():
        pltpu.make_async_copy(out, out, recv_sem.at[3]).wait()


def per_device(previous, stale_keys, stale_values, modulation, q_gain, k_gain, blocks, refresh):
    sections = lax.axis_size("section")
    patches = lax.axis_size("patch")
    _, tok_rows, width = previous.shape
    _, layers, tokens, _ = stale_keys.shape
    head = q_gain.shape[-1]
    part = width // WORKERS
    anywhere = pl.BlockSpec(memory_space=pl.ANY)
    operands = (previous, stale_keys, stale_values, jnp.swapaxes(modulation, 1, 2), q_gain, k_gain, refresh)
    stay = [pltpu.with_memory_space_constraint(operand, pltpu.HBM) for operand in operands]
    mixed = pl.pallas_call(
        functools.partial(kernel, sections, patches, head),
        out_shape=pltpu.VMEM((tok_rows, width), jnp.bfloat16),
        in_specs=[anywhere] * 8,
        out_specs=pl.BlockSpec(memory_space=pltpu.VMEM),
        scratch_shapes=[
            pltpu.VMEM((tok_rows, width), jnp.bfloat16),
            pltpu.VMEM((1, 128), jnp.float32),
            pltpu.VMEM((tokens, part), jnp.bfloat16),
            pltpu.VMEM((patches, 1, 128), jnp.float32),
            pltpu.VMEM((layers, tokens, part), jnp.bfloat16),
            pltpu.VMEM((layers, tokens, part), jnp.bfloat16),
            pltpu.VMEM((3, layers, part), jnp.float32),
            pltpu.VMEM((layers, head), jnp.float32),
            pltpu.VMEM((layers, head), jnp.float32),
            pltpu.VMEM((1, patches), jnp.int32),
            pltpu.VMEM((1, 1), jnp.int32),
            pltpu.VMEM((tokens // 128, 128), jnp.float32),
            pltpu.VMEM((WORKERS, tokens // 128, 128), jnp.float32),
            pltpu.VMEM((tokens, part), jnp.bfloat16),
            pltpu.SemaphoreType.DMA((9,)),
            pltpu.SemaphoreType.DMA((4,)),
            pltpu.SemaphoreType.DMA((4 + PIECES,)),
            pltpu.SemaphoreType.REGULAR,
        ],
        compiler_params=pltpu.CompilerParams(
            collective_id=0, has_side_effects=True, vmem_limit_bytes=VMEM_BYTES
        ),
    )(*stay, blocks[None])
    return mixed.astype(jnp.float32)[None]


def solution(mesh):
    placed = (
        P("section", "patch", None),
        P("section", None, None, None),
        P("section", None, None, None),
        P("section", None, None, None),
        P("section", None, None),
        P("section", None, None),
        P("section"),
        P("section", None),
    )
    return jax.shard_map(
        per_device,
        mesh=mesh,
        in_specs=placed,
        out_specs=P("section", "patch", None),
        check_vma=False,
    )
```
